128 devices in a mesh: blk: 8 (over y, core), sector: 16 (over x, z).
Axes of the slice: x: 4, y: 4, z: 4, core: 2. Of those that a mesh axis runs over, the one named last changes fastest.
Arguments:
- local_gap: float32 [8, 16, 64, 2048], P('blk', 'sector'), may hold values from -6 to 6
- previous: float32 [8, 16, 64, 2048], P('blk', 'sector'), may hold values from -6 to 6
- flexibility: bfloat16 [8, 16, 2048, 2048], P('blk', 'sector'), as said below
- schur: bfloat16 [8, 16, 2048, 2048], P('blk', 'sector'), as said below
- corner_flex: bfloat16 [8, 16, 24, 2048], P('blk', 'sector'), may hold values from -0.375 to 0.375
- coarse_inverse: float32 [864, 864], P('sector'), as said below
- scaling: float32 [8, 16, 2048], P('blk', 'sector'), may hold values from 0.2 to 2
- counts: int32 [8, 16, 4], P('blk', 'sector'), may hold values from 0 to 512, as said below
- matching: int32 [8, 16, 2048], P('blk', 'sector'), may hold values from 0 to 511, as said below
- corner_map: int32 [8, 16, 24], P('blk', 'sector'), may hold values from 0 to 863, as said below
Outputs:
- multipliers: float32 [8, 16, 64, 2048], P('blk', 'sector')
- residual: float32 [8, 16, 64, 2048], P('blk', 'sector')
- precond: float32 [8, 16, 64, 2048], P('blk', 'sector')
The draws below stay inside these ranges and needn't reach their ends.
Inputs may be any that keep to these rules, and one draw needn't show every extreme that they name: `counts`: every face shared by two subdomains has between 128 and 512 slots in use, the same number on both sides; the lower face of the first cycle and the upper face of the last cycle have none; some face has exactly 512. On every face the slots in use are matched one to one with the slots in use of the neighbour's opposite face, and the neighbour's matching is the inverse of this one; slots not in use hold some index of the face. `corner_map`: component q of the corner node that subdomains share maps to the same coarse dof in each of them; the numbering of all corner nodes' components is one to one onto 0 to 863. `flexibility`: symmetric positive definite for every subdomain. `schur`: symmetric positive definite for every subdomain. `coarse_inverse`: symmetric positive definite.
All inputs are finite; a program needn't handle non-finite values.
Results may differ from the reference program's by a relative error of at most 0.0065.
The reference program's roundings to bfloat16 on the way (of `rounded`, `back` and `scaled`) count: a program that leaves them out, or rounds other values in their place, can miss the bound.
Values sent between devices are 32-bit elements; how exact they have to be, the bound alone decides.
No kernel may reach another device: no remote copies, remote signals or barrier semaphores. Data moves between devices by JAX's collectives and lax.ppermute only.
A program may use at most 128 MiB of HBM per device.

```python
import math
import jax
import jax.numpy as jnp
from jax import lax

FMAX = 512
NI = 2048
R = 64
COMP = 3
CL = 24
ITERS = 2
CYCLES = 8
SECTORS = 16
NCG = 864


def interface_pairs(key):
    axial = jax.random.randint(jax.random.fold_in(key, 1), (CYCLES, SECTORS), FMAX // 4, FMAX + 1)
    beside_all = jax.random.randint(jax.random.fold_in(key, 2), (CYCLES, SECTORS), FMAX // 4, FMAX + 1)
    beside_all = beside_all.at[0, 0].set(FMAX)
    positions = jnp.arange(FMAX)

    def ordering(count_table, subkey):
        scores = jax.random.randint(subkey, (CYCLES, SECTORS, FMAX), 0, 2 ** 18) * FMAX + positions
        scores = jnp.where(positions < count_table[:, :, None], scores, 2 ** 30 + positions)
        return jnp.argsort(scores, axis=-1).astype(jnp.int32)
    axial_perm = ordering(axial, jax.random.fold_in(key, 3))
    around_perm = ordering(beside_all, jax.random.fold_in(key, 4))
    return (axial.astype(jnp.int32), beside_all.astype(jnp.int32), axial_perm, around_perm)


def draw_counts(key, part):
    axial, beside_all, axial_perm, around_perm = interface_pairs(jax.random.fold_in(key, 11))
    cycle = jnp.arange(CYCLES)[:, None]
    face_lower = jnp.where(cycle > 0, jnp.roll(axial, 1, axis=0), 0)
    face_upper = jnp.where(cycle < CYCLES - 1, axial, 0)
    face_prev = jnp.roll(beside_all, 1, axis=1)
    return jnp.stack([face_lower, face_upper, face_prev, beside_all], axis=-1).astype(jnp.int32)


def draw_matching(key, part):
    axial, beside_all, axial_perm, around_perm = interface_pairs(jax.random.fold_in(key, 11))
    axial_back = jnp.argsort(axial_perm, axis=-1).astype(jnp.int32)
    around_back = jnp.argsort(around_perm, axis=-1).astype(jnp.int32)
    face_lower = jnp.roll(axial_back, 1, axis=0)
    face_prev = jnp.roll(around_back, 1, axis=1)
    return jnp.concatenate([face_lower, axial_perm, face_prev, around_perm], axis=-1).astype(jnp.int32)


def draw_corner_map(key, part):
    numbering = jax.random.permutation(jax.random.fold_in(key, 5), NCG).astype(jnp.int32)
    cycle = jnp.arange(CYCLES)[:, None, None]
    sector = jnp.arange(SECTORS)[None, :, None]
    corner = jnp.arange(8 * COMP)[None, None, :]
    axial = corner // (4 * COMP)
    circular = corner // (2 * COMP) % 2
    radial = corner // COMP % 2
    component = corner % COMP
    natural = (((cycle + axial) * SECTORS + (sector + circular) % SECTORS) * 2 + radial) * COMP + component
    return numbering[natural].astype(jnp.int32)


def definite_matrix(subkey, order, diag_lo, diag_hi):
    raw = jax.random.uniform(jax.random.fold_in(subkey, 1), (order, order), jnp.float32, -1.0, 1.0)
    symmetric = 0.5 * (raw + raw.T)
    distance = jnp.abs(jnp.arange(order)[:, None] - jnp.arange(order)[None, :])
    dense_level = 0.6 / math.sqrt(order)
    decay = jnp.where(distance > 0, 0.18 / jnp.maximum(distance, 1).astype(jnp.float32) ** 1.5 + dense_level, 0.0)
    diagonal = jax.random.uniform(jax.random.fold_in(subkey, 2), (order,), jnp.float32, diag_lo, diag_hi)
    matrix = symmetric * decay + jnp.diag(diagonal)
    return matrix


def subdomain_matrices(key, diag_lo, diag_hi):
    keys = jax.random.split(key, CYCLES * SECTORS)
    stacked = lax.map(lambda subkey: definite_matrix(subkey, NI, diag_lo, diag_hi).astype(jnp.bfloat16), keys)
    return stacked.reshape(CYCLES, SECTORS, NI, NI)


def draw_flexibility(key, part):
    return subdomain_matrices(jax.random.fold_in(key, 21), 1.0, 1.5)


def draw_schur(key, part):
    return subdomain_matrices(jax.random.fold_in(key, 22), 1.0, 2.0)


def draw_coarse_inverse(key, part):
    return 0.3 * definite_matrix(jax.random.fold_in(key, 23), NCG, 1.0, 3.0)


def block_scale(key, extent, cuts, smallest, top_value):
    factor_of = 1.0
    for dim, blocks in cuts:
        heights = jax.random.uniform(jax.random.fold_in(jax.random.fold_in(key, 6), dim), (blocks,), jnp.float32, smallest / len(cuts), top_value / len(cuts))
        factor_of = factor_of * jnp.repeat(jnp.exp(heights), extent[dim] // blocks).reshape((-1,) + (1,) * (len(extent) - 1 - dim))
    return factor_of


def noise(key, extent, scale, reach, cuts=(), held_as=jnp.bfloat16):
    factor_of = block_scale(key, extent, cuts, -0.22, 0.18) if cuts else 1.0
    array = jax.random.normal(key, extent, jnp.float32) * scale * factor_of
    return jnp.minimum(jnp.maximum(array, -reach), reach).astype(held_as)


def setup_inputs(seed: int = 0) -> dict:
    splits = jax.random.split(jax.random.key(seed), 11)
    local_gap = noise(splits[0], (CYCLES, SECTORS, R, NI), 1.0, 6.0, ((0, 8), (1, 16)), jnp.float32)
    previous = noise(splits[1], (CYCLES, SECTORS, R, NI), 1.0, 6.0, ((0, 8), (1, 16)), jnp.float32)
    flexibility = draw_flexibility(jax.random.fold_in(splits[10], 71), 0)
    schur = draw_schur(jax.random.fold_in(splits[10], 71), 0)
    corner_flex = noise(splits[4], (CYCLES, SECTORS, CL, NI), (NI // 8) ** -0.5, 0.375, ((0, 8), (1, 16)))
    coarse_inverse = draw_coarse_inverse(jax.random.fold_in(splits[10], 71), 0)
    scaling = jnp.clip(jnp.exp(math.log(2.0) - 2.3025851 * jax.random.uniform(splits[6], (CYCLES, SECTORS, NI), jnp.float32) ** block_scale(splits[6], (CYCLES, SECTORS, NI), ((0, 8), (1, 16)), -0.2, 0.2)), 0.2, 2.0)
    counts = draw_counts(jax.random.fold_in(splits[10], 71), 0)
    matching = draw_matching(jax.random.fold_in(splits[10], 71), 0)
    corner_map = draw_corner_map(jax.random.fold_in(splits[10], 71), 0)
    return dict(local_gap=local_gap, previous=previous, flexibility=flexibility, schur=schur, corner_flex=corner_flex, coarse_inverse=coarse_inverse, scaling=scaling, counts=counts, matching=matching, corner_map=corner_map)


def pair_map(function, first, second):
    leading = first.shape[:2]
    result = lax.map(lambda pair: function(pair[0], pair[1]), (first.reshape((-1,) + first.shape[2:]), second.reshape((-1,) + second.shape[2:])))
    return result.reshape(leading + result.shape[1:])


def times_matrix(vector, matrix):
    return jnp.dot(vector, matrix, preferred_element_type=jnp.float32)


def times_transpose(vector, matrix):
    return jnp.dot(vector, matrix.T, preferred_element_type=jnp.float32)


def jump(field, matching, active):
    cycles, sectors, rows, width = field.shape
    face_size = width // 4
    faces = field.reshape(cycles, sectors, rows, 4, face_size)
    zeros = jnp.zeros_like(faces[:1, :, :, 1])
    from_lower = jnp.concatenate([zeros, faces[:-1, :, :, 1]], axis=0)
    from_upper = jnp.concatenate([faces[1:, :, :, 0], zeros], axis=0)
    from_prev = jnp.roll(faces[:, :, :, 3], 1, axis=1)
    from_next = jnp.roll(faces[:, :, :, 2], -1, axis=1)
    beside = jnp.stack([from_lower, from_upper, from_prev, from_next], axis=3)
    index = jnp.broadcast_to(matching.reshape(cycles, sectors, 1, 4, face_size), beside.shape)
    picked = jnp.take_along_axis(beside, index, axis=4)
    masked = (faces - picked) * active.reshape(cycles, sectors, 1, 4, face_size)
    return masked.reshape(cycles, sectors, rows, width)


def apply_operator(field, flexibility, corner_flex, coarse_inverse, onehot):
    rounded = field.astype(jnp.bfloat16)
    local = pair_map(times_matrix, rounded, flexibility)
    corner_part = pair_map(times_transpose, rounded, corner_flex)
    spread = jnp.einsum("bsrk,bskn->rn", corner_part, onehot, precision=lax.Precision.HIGHEST)
    coarse = jnp.dot(spread, coarse_inverse, precision=lax.Precision.HIGHEST, preferred_element_type=jnp.float32)
    back = jnp.einsum("rn,bskn->bsrk", coarse, onehot, precision=lax.Precision.HIGHEST).astype(jnp.bfloat16)
    return local + pair_map(times_matrix, back, corner_flex)


def precondition(residual, schur, scaling, matching, active):
    weights = scaling[:, :, None, :]
    scaled = (residual * weights).astype(jnp.bfloat16)
    product = pair_map(times_matrix, scaled, schur)
    return jump(product * weights, matching, active)


def reference(local_gap, previous, flexibility, schur, corner_flex, coarse_inverse, scaling, counts, matching, corner_map):
    face_size = local_gap.shape[3] // 4
    active = (jnp.arange(face_size)[None, None, None, :] < counts[:, :, :, None]).astype(jnp.float32)
    active = active.reshape(counts.shape[0], counts.shape[1], 4 * face_size)
    onehot = (corner_map[:, :, :, None] == jnp.arange(NCG)[None, None, None, :]).astype(jnp.float32)
    start = 0.5 * jump(previous, matching, active)
    residual = jump(local_gap - apply_operator(start, flexibility, corner_flex, coarse_inverse, onehot), matching, active)
    precond = precondition(residual, schur, scaling, matching, active)
    direction = precond
    multipliers = start
    energy = jnp.sum(residual * precond, axis=(0, 1, 3))
    for step in range(ITERS):
        image = jump(apply_operator(direction, flexibility, corner_flex, coarse_inverse, onehot), matching, active)
        curvature = jnp.sum(direction * image, axis=(0, 1, 3))
        alpha = (energy / curvature)[None, None, :, None]
        multipliers = multipliers + alpha * direction
        residual = residual - alpha * image
        precond = precondition(residual, schur, scaling, matching, active)
        if step + 1 < ITERS:
            fresh = jnp.sum(residual * precond, axis=(0, 1, 3))
            direction = precond + (fresh / energy)[None, None, :, None] * direction
            energy = fresh
    return multipliers, residual, precond
```

```python
import jax
import jax.numpy as jnp
from jax import lax
from jax.sharding import PartitionSpec as P

ITERS = 2
BOTH = ("blk", "sector")
PAYLOAD = 16


def swap(block, axis, offset):
    count = lax.axis_size(axis)
    route = []
    for i in range(offset, count + offset, 2):
        one, two = i % count, (i + 1) % count
        route += [(one, two), (two, one)]
    return lax.ppermute(block, axis, route)


def split_parts(x, parts):
    out = []
    for _ in range(parts):
        head = lax.reduce_precision(x, 8, 7)
        out.append(head.astype(jnp.bfloat16))
        x = x - head
    return out


def core_groups(blk, sector):
    return [[b * sector + s for b in range(c, blk, 2) for s in range(sector)] for c in range(2)]


def body(
    local_gap,
    previous,
    flexibility,
    schur,
    corner_flex,
    coarse_inverse,
    scaling,
    counts,
    matching,
    corner_map,
):
    f32, bf16 = jnp.float32, jnp.bfloat16
    gap = local_gap[0, 0]
    prior = previous[0, 0]
    flex = flexibility[0, 0]
    dirichlet = schur[0, 0]
    corners = corner_flex[0, 0]
    weights = scaling[0, 0][None, :]
    rows, width = gap.shape
    face = width // 4
    corner_count = corners.shape[0]
    half = corner_count // 2
    coarse_count = coarse_inverse.shape[1]
    blk, sector = lax.axis_size("blk"), lax.axis_size("sector")
    groups = core_groups(blk, sector)
    members = len(groups[0])
    odd_b = lax.rem(lax.axis_index("blk"), 2) == 1
    odd_s = lax.rem(lax.axis_index("sector"), 2) == 1
    highest = lax.Precision.HIGHEST
    high = lax.Precision.HIGH

    full_inverse = lax.all_gather(coarse_inverse, "sector", axis=0, tiled=True)

    active = (jnp.arange(face)[None, :] < counts[0, 0][:, None]).astype(f32)
    match_faces = matching[0, 0].reshape(4, face)
    picker = (jnp.arange(face)[None, :, None] == match_faces[:, None, :]).astype(f32)
    picker = (picker * active[:, None, :]).astype(bf16)
    active_row = active.reshape(1, width)

    def to_links(faces):
        low, up, prev, foll = faces
        return (
            jnp.where(odd_b, low, up),
            jnp.where(odd_b, up, low),
            jnp.where(odd_s, prev, foll),
            jnp.where(odd_s, foll, prev),
        )

    def from_links(links):
        b0, b1, s0, s1 = links
        return (
            jnp.where(odd_b, b0, b1),
            jnp.where(odd_b, b1, b0),
            jnp.where(odd_s, s0, s1),
            jnp.where(odd_s, s1, s0),
        )

    def exchange(faces):
        b0, b1, s0, s1 = to_links(faces)
        s1 = swap(s1, "sector", 1)
        s0 = swap(s0, "sector", 0)
        b1 = swap(b1, "blk", 1)
        b0 = swap(b0, "blk", 0)
        return from_links((b0, b1, s0, s1))

    def faces_of(field):
        return [field[:, f * face : (f + 1) * face] for f in range(4)]

    def pick(blocks):
        out = []
        for f in range(4):
            parts = split_parts(blocks[f], 3)
            stacked = jnp.concatenate(parts, axis=0)
            got = jnp.dot(stacked, picker[f], preferred_element_type=f32)
            n = blocks[f].shape[0]
            out.append(got[:n] + got[n : 2 * n] + got[2 * n :])
        return out

    def jump(field):
        picked = pick(exchange(faces_of(field)))
        return field * active_row - jnp.concatenate(picked, axis=1)

    own_map = corner_map[0, 0].astype(f32)
    map_row = jnp.zeros((8, face), f32).at[0, :corner_count].set(own_map)
    corners32 = corners.astype(f32)
    sent = [
        jnp.concatenate([p, c, map_row], axis=0)
        for p, c in zip(faces_of(prior), faces_of(corners32))
    ]
    came = exchange(sent)
    picked = pick([block[:rows] for block in came])
    start = 0.5 * (prior * active_row - jnp.concatenate(picked, axis=1))
    corner_faces = []
    maps = [own_map]
    for f in range(4):
        own = corners32[:, f * face : (f + 1) * face] * active[f][None, :]
        theirs = jnp.dot(
            came[f][rows : rows + corner_count].astype(bf16),
            picker[f],
            preferred_element_type=f32,
        )
        corner_faces.append(jnp.concatenate([own, -theirs], axis=0).astype(bf16))
        maps.append(came[f][rows + corner_count, :corner_count])
    numbers = jnp.arange(coarse_count).astype(f32)
    taken = (jnp.concatenate(maps)[None, :] == numbers[:, None]).astype(f32)

    def product(vector, matrix):
        return jnp.dot(vector, matrix, preferred_element_type=f32)

    def corner_parts(rounded):
        return lax.dot_general(
            corners, rounded, (((1,), (1,)), ((), ())), preferred_element_type=f32
        )

    def gather(part, scalars):
        body_rows = jnp.concatenate([part[:half], part[half:]], axis=1)
        rest = [jnp.pad(s.reshape(1, -1), ((0, 0), (0, 2 * rows - s.size))) for s in scalars]
        pad = jnp.zeros((PAYLOAD - half - len(rest), 2 * rows), f32)
        payload = jnp.concatenate([body_rows] + rest + [pad], axis=0)
        many = jnp.broadcast_to(payload[None], (members,) + payload.shape)
        many = many.reshape(members * PAYLOAD, 2 * rows)
        got = lax.all_to_all(
            many, BOTH, split_axis=0, concat_axis=0, tiled=True, axis_index_groups=groups
        )
        return got.reshape(members, PAYLOAD, 2 * rows)

    def assemble(got, spots, scalar_rows):
        lower = got[:, :half, :rows].reshape(members * half, rows)
        upper = got[:, :half, rows:].reshape(members * half, rows)
        both = jnp.concatenate([lower, upper], axis=0)
        stacked = jnp.concatenate(split_parts(both, 3), axis=1)
        sums = lax.dot_general(
            stacked, spots, (((0,), (0,)), ((), ())), preferred_element_type=f32
        )
        spread = sums[:rows] + sums[rows : 2 * rows] + sums[2 * rows :]
        scalars = jnp.sum(got[:, half : half + 1 + scalar_rows], axis=0)
        scalars = jnp.pad(scalars, ((0, 7 - scalar_rows), (0, coarse_count - 2 * rows)))
        mine = jnp.concatenate([spread, scalars], axis=0)
        mine = mine + swap(mine, "blk", 0)
        return mine[:rows], mine[rows:]

    def solve_coarse(spread):
        coarse = jnp.dot(spread, full_inverse, precision=high, preferred_element_type=f32)
        quad = jnp.sum(spread * coarse, axis=1)
        head = jnp.concatenate(split_parts(coarse, 3), axis=0)
        back = jnp.dot(head, taken.astype(bf16), preferred_element_type=f32)
        back = (back[:rows] + back[rows : 2 * rows] + back[2 * rows :]).astype(bf16)
        out = []
        for f in range(4):
            own = back[:, :corner_count]
            theirs = back[:, (f + 1) * corner_count : (f + 2) * corner_count]
            out.append(product(jnp.concatenate([own, theirs], axis=1), corner_faces[f]))
        return jnp.concatenate(out, axis=1), quad

    def preconditioned(residual):
        scaled = (residual * weights).astype(bf16)
        return product(scaled, dirichlet) * weights

    rounded = start.astype(bf16)
    got = gather(corner_parts(rounded), [own_map])
    field = jump(gap - product(rounded, flex))
    places = got[:, half, :corner_count]
    places = jnp.concatenate([places[:, :half].reshape(-1), places[:, half:].reshape(-1)])
    spots = (places[:, None] == numbers[None, :]).astype(bf16)
    spread, _ = assemble(got, spots, 0)
    behind, _ = solve_coarse(spread)
    residual = field - behind

    weighted = preconditioned(residual)
    energy = jnp.sum(residual * weighted, axis=1)
    direction = jump(weighted)
    rounded = direction.astype(bf16)
    local = product(rounded, flex)
    inner = jnp.sum(direction * local, axis=1)
    got = gather(corner_parts(rounded), [jnp.concatenate([energy, inner])])
    image_local = jump(local)
    spread, scalars = assemble(got, spots, 0)
    behind, quad = solve_coarse(spread)
    energy, inner = scalars[0, :rows], scalars[0, rows : 2 * rows]
    alpha = (energy / (inner + quad))[:, None]
    multipliers = start + alpha * direction
    residual = residual - alpha * (image_local + behind)

    weighted = preconditioned(residual)
    fresh = jnp.sum(residual * weighted, axis=1)
    precond = jump(weighted)
    parts = jnp.concatenate(split_parts(precond, 2), axis=0)
    local_2 = product(parts, flex)
    local_2 = local_2[:rows] + local_2[rows:]
    part = corner_parts(parts)
    part = part[:, :rows] + part[:, rows:]
    inner_2 = jnp.sum(precond * local_2, axis=1)
    cross = jnp.sum(precond * local, axis=1)
    got = gather(part, [jnp.concatenate([fresh, inner_2]), cross])
    image_2 = jump(local_2)
    spread_2, scalars = assemble(got, spots, 1)
    fresh, inner_2 = scalars[0, :rows], scalars[0, rows : 2 * rows]
    cross = scalars[1, :rows]
    beta = fresh / energy
    behind, quad = solve_coarse(spread_2 + beta[:, None] * spread)
    inner = inner_2 + beta * (2.0 * cross + beta * inner)
    alpha = (fresh / (inner + quad))[:, None]
    beta = beta[:, None]
    direction = precond + beta * direction
    multipliers = multipliers + alpha * direction
    residual = residual - alpha * (image_2 + beta * image_local + behind)
    precond = jump(preconditioned(residual))
    return (multipliers[None, None], residual[None, None], precond[None, None])


def solution(mesh):
    field = P("blk", "sector", None, None)
    vector = P("blk", "sector", None)
    placed = (field, field, field, field, field, P("sector", None), vector, vector, vector, vector)
    return jax.shard_map(
        body,
        mesh=mesh,
        in_specs=placed,
        out_specs=(field, field, field),
        check_vma=False,
    )
```

```python
import functools

import jax
import jax.numpy as jnp
from jax import lax
from jax.experimental import pallas as pl
from jax.experimental.pallas import tpu as pltpu
from jax.sharding import PartitionSpec as P

BOTH = ("blk", "sector")
PAYLOAD = 16
LANES = 128
SPAN = 32
F32, BF16 = jnp.float32, jnp.bfloat16
VMEM_LIMIT = 12 * 1024 * 1024


def swap(block, axis, offset):
    count = lax.axis_size(axis)
    route = []
    for i in range(offset, count + offset, 2):
        one, two = i % count, (i + 1) % count
        route += [(one, two), (two, one)]
    return lax.ppermute(block, axis, route)


def core_groups(blk, sector):
    return [[b * sector + s for b in range(c, blk, 2) for s in range(sector)] for c in range(2)]


def parts_of(x, count):
    out = []
    for _ in range(count):
        head = x.astype(BF16)
        out.append(head)
        x = x - head.astype(F32)
    return out


def dot(a, b):
    return jnp.dot(a, b, preferred_element_type=F32)


def dot_nt(a, b):
    return lax.dot_general(a, b, (((1,), (1,)), ((), ())), preferred_element_type=F32)


def dot_tn(a, b):
    return lax.dot_general(a, b, (((0,), (0,)), ((), ())), preferred_element_type=F32)


def columns(order, link, face):
    return pl.ds(pl.multiple_of(order[link] * face, face), face)


def picked(came, picker, link, rows):
    stacked = jnp.concatenate(parts_of(came[link][0:rows, :], 3), axis=0)
    got = dot(stacked, picker[link])
    return got[:rows] + got[rows : 2 * rows] + got[2 * rows :]


def column(row, rows):
    return jnp.transpose(jnp.broadcast_to(row, (LANES, LANES)))[:rows]


def take_rows(taken, which, row):
    number = column(row, SPAN)
    lane = lax.broadcasted_iota(jnp.int32, (SPAN, LANES), 1).astype(F32)
    for at in range(0, taken.shape[1], LANES):
        hit = jnp.where(number == lane + float(at), 1.0, 0.0)
        taken[which * SPAN : (which + 1) * SPAN, at : at + LANES] = hit.astype(BF16)


def flex_kernel(mode, order, *refs):
    refs = list(refs)
    came = [refs.pop(0) for _ in range(4)]
    field, picker, active, flex, corners = [refs.pop(0) for _ in range(5)]
    if mode == 0:
        gap, extra, numbers = refs.pop(0), refs.pop(0), refs.pop(0)
    if mode >= 1:
        energy = refs.pop(0)
    if mode == 2:
        old = refs.pop(0)
    p_out, h_out = refs.pop(0), refs.pop(0)
    links = [refs.pop(0) for _ in range(4)]
    if mode == 0:
        corner_faces, taken = refs.pop(1), refs.pop(1)
    payload, stack = refs
    rows, width = field.shape
    face = width // 4
    for link in range(4):
        cols = columns(order, link, face)
        p = field[:, cols] * active[:, cols] - picked(came, picker, link, rows)
        if mode == 0:
            p = 0.5 * p
        p_out[:, cols] = p
        if mode == 2:
            head, rest = parts_of(p, 2)
            stack[0:rows, cols] = head
            stack[rows : 2 * rows, cols] = rest
        else:
            stack[:, cols] = p.astype(BF16)
    if mode == 0:
        take_rows(taken, 0, numbers[0:1, 0:LANES])
        for link in range(4):
            cols = columns(order, link, face)
            own = corners[:, cols].astype(F32) * active[:, cols]
            theirs = dot(came[link][rows : rows + SPAN, :].astype(BF16), picker[link])
            corner_faces[link, 0:SPAN, :] = own.astype(BF16)
            corner_faces[link, SPAN : 2 * SPAN, :] = (-theirs).astype(BF16)
            take_rows(taken, link + 1, came[link][rows + SPAN : rows + SPAN + 1, 0:LANES])
    part = dot_nt(corners[...], stack[...])
    inner = jnp.zeros((rows, 1), F32)
    cross = jnp.zeros((rows, 1), F32)
    for link in range(4):
        cols = columns(order, link, face)
        local = dot(stack[...], flex[:, cols])
        if mode == 2:
            local = local[:rows] + local[rows:]
        p = p_out[:, cols]
        if mode == 0:
            local = gap[:, cols] - local
        else:
            inner = inner + jnp.sum(p * local, axis=1, keepdims=True)
        if mode == 2:
            cross = cross + jnp.sum(p * old[:, cols], axis=1, keepdims=True)
        h_out[:, cols] = local
        links[link][...] = local
    if mode == 2:
        part = part[:, :rows] + part[:, rows:]
    payload[0:16, 0:rows] = part[0:16]
    payload[0:8, rows : 2 * rows] = part[16:24]
    if mode == 0:
        scalars = extra[...]
    else:
        lane = lax.broadcasted_iota(jnp.int32, (rows, LANES), 1)
        table = jnp.where(lane == 0, energy[...], jnp.where(lane == 1, inner, 0.0))
        table = jnp.where(lane == 2, cross, table)
        scalars = jnp.transpose(table)[0:8]
    payload[8:16, rows : 2 * rows] = scalars


def first_kernel(order, prior, corners, numbers, *links):
    rows, width = prior.shape
    face = width // 4
    for link in range(4):
        cols = columns(order, link, face)
        links[link][0:rows, :] = prior[:, cols]
        links[link][rows : rows + SPAN, :] = corners[:, cols].astype(F32)
        links[link][rows + SPAN :, :] = numbers[...]


def picker_kernel(order, matching, active, flex, dirichlet, picker):
    face = picker.shape[1]
    source = lax.broadcasted_iota(jnp.int32, (face, face), 0)
    for link in range(4):
        cols = columns(order, link, face)
        hit = (source == matching[:, cols]) & (active[:, cols] > 0.5)
        picker[link] = jnp.where(hit, 1.0, 0.0).astype(BF16)


def assemble_kernel(mode, *refs):
    if mode == 0:
        got, places, out, spots = refs[0], refs[1], refs[-2], refs[-1]
        count = spots.shape[1]
        source = lax.broadcasted_iota(jnp.int32, (LANES, got.shape[0]), 0)
        for which in range(2):
            for at in range(0, count, LANES):
                hit = source + at == places[which : which + 1, :]
                spots[which, at : at + LANES, :] = jnp.where(hit, 1.0, 0.0).astype(BF16)
    else:
        got, spots, out = refs[0], refs[1], refs[-1]
    members = got.shape[0] // PAYLOAD
    half = spots.shape[1] // 2
    both = jnp.concatenate(parts_of(got[...], 2), axis=1)
    low = dot(spots[0], both)
    high = dot(spots[1], both)
    low = low[:, :LANES] + low[:, LANES:]
    high = high[:, :LANES] + high[:, LANES:]
    spread = low + pltpu.roll(high, LANES // 2, 1)
    lane = lax.broadcasted_iota(jnp.int32, (half, LANES), 1)
    out[0:half, :] = jnp.where(
        lane < LANES // 2, spread[:half], pltpu.roll(spread[half:], LANES // 2, 1)
    )
    total = jnp.sum(got[...].reshape(members, PAYLOAD, LANES), axis=0)
    out[half : half + 8, :] = total[8:16]


def coarse_kernel(mode, *refs):
    refs = list(refs)
    mine, theirs, taken = refs.pop(0), refs.pop(0), refs.pop(0)
    if mode == 0:
        inverse, back_out, head, rest = refs
        for at in range(0, inverse.shape[0], LANES):
            one, two = parts_of(inverse[at : at + LANES, :], 2)
            head[at : at + LANES, :] = one
            rest[at : at + LANES, :] = two
    else:
        head, rest = refs.pop(0), refs.pop(0)
    if mode == 1:
        back_out, alpha_out, spread_out, sums_out = refs
    if mode == 2:
        spread_old, sums_old, back_out, alpha_out, beta_out = refs
    rows = LANES // 2
    count = taken.shape[1]
    half = count // 2
    shift = LANES // 2
    total = mine[...] + theirs[...]
    spread = jnp.concatenate([total[:half], pltpu.roll(total[:half], shift, 1)], axis=0)
    sums = pltpu.roll(total[half:], shift, 1)
    valid = lax.broadcasted_iota(jnp.int32, (count, LANES), 1) < shift
    valid_row = lax.broadcasted_iota(jnp.int32, (1, LANES), 1) < shift
    spread = jnp.where(valid, spread, 0.0)
    if mode >= 1:
        energy, inner = sums[0:1], sums[1:2]
    if mode == 1:
        spread_out[...] = spread
        sums_out[...] = sums
    if mode == 2:
        beta = jnp.where(valid_row, energy / sums_old[0:1, :], 0.0)
        spread = spread + beta * spread_old[...]
        inner = inner + beta * (2.0 * sums[2:3] + beta * sums_old[1:2, :])
        beta_out[...] = column(beta, rows)
    first = spread.astype(BF16)
    second = spread - first.astype(F32)
    pair = (first.astype(F32) + pltpu.roll(second, shift, 1)).astype(BF16)
    coarse = dot(head[...], pair)
    coarse = coarse + pltpu.roll(coarse, shift, 1) + dot(rest[...], first)
    coarse = jnp.where(valid, coarse, 0.0)
    if mode >= 1:
        quad = jnp.sum(spread * coarse, axis=0, keepdims=True)
        alpha_out[...] = column(jnp.where(valid_row, energy / (inner + quad), 0.0), rows)
    one, two, three = parts_of(coarse, 3)
    pair = (one.astype(F32) + pltpu.roll(two.astype(F32), shift, 1)).astype(BF16)
    back = dot(taken[...], jnp.concatenate([pair, three], axis=1))
    low = back[:, :LANES]
    back_out[...] = low + pltpu.roll(low, shift, 1) + back[:, LANES:]


def schur_kernel(mode, order, *refs):
    refs = list(refs)
    back = refs.pop(0)
    came = [refs.pop(0) for _ in range(4)]
    field, picker, active, corner_faces, dirichlet, weights = [refs.pop(0) for _ in range(6)]
    if mode >= 1:
        alpha, before, direction, multipliers = [refs.pop(0) for _ in range(4)]
        alpha = alpha[:, 0:1]
    if mode == 2:
        beta, image_old, old = [refs.pop(0) for _ in range(3)]
        beta = beta[:, 0:1]
    residual, weighted = refs.pop(0), refs.pop(0)
    links = [refs.pop(0) for _ in range(4)]
    if mode <= 1:
        energy_out = refs.pop(0)
    if mode >= 1:
        mult_out = refs.pop(0)
    if mode == 1:
        image_out = refs.pop(0)
    (scaled,) = refs
    rows, width = field.shape
    face = width // 4
    back = back[...][:, :rows].astype(BF16)

    for link in range(4):
        cols = columns(order, link, face)
        jumped = field[:, cols] * active[:, cols] - picked(came, picker, link, rows)
        pieces = [back[0:SPAN], back[(link + 1) * SPAN : (link + 2) * SPAN]]
        behind = dot_tn(jnp.concatenate(pieces, axis=0), corner_faces[link])
        if mode == 0:
            now = jumped - behind
        else:
            d = direction[:, cols]
            if mode == 1:
                image_out[:, cols] = jumped
            else:
                jumped = jumped + beta * image_old[:, cols]
                d = d + beta * old[:, cols]
            mult_out[:, cols] = multipliers[:, cols] + alpha * d
            now = before[:, cols] - alpha * (jumped + behind)
        residual[:, cols] = now
        scaled[:, cols] = (now * weights[:, cols]).astype(BF16)
    energy = jnp.zeros((rows, 1), F32)
    for link in range(4):
        cols = columns(order, link, face)
        w = dot(scaled[...], dirichlet[:, cols]) * weights[:, cols]
        weighted[:, cols] = w
        links[link][...] = w
        if mode <= 1:
            energy = energy + jnp.sum(residual[:, cols] * w, axis=1, keepdims=True)
    if mode <= 1:
        energy_out[...] = jnp.broadcast_to(energy, (rows, LANES))


def last_kernel(order, *refs):
    came, (field, picker, active, out) = refs[:4], refs[4:]
    rows, width = field.shape
    for link in range(4):
        cols = columns(order, link, width // 4)
        out[:, cols] = field[:, cols] * active[:, cols] - picked(came, picker, link, rows)


def call(kernel, order, arrays, shapes, scratch=(), flops=0):
    where = pl.BlockSpec(memory_space=pltpu.VMEM)
    moved = sum(a.size * a.dtype.itemsize for a in arrays)
    return pl.pallas_call(
        kernel,
        out_shape=[s if hasattr(s, "dtype") else jax.ShapeDtypeStruct(s, F32) for s in shapes],
        in_specs=[pl.BlockSpec(memory_space=pltpu.SMEM)] * len(order) + [where] * len(arrays),
        out_specs=[where] * len(shapes),
        scratch_shapes=list(scratch),
        compiler_params=pltpu.CompilerParams(vmem_limit_bytes=VMEM_LIMIT),
        cost_estimate=pl.CostEstimate(flops=flops, bytes_accessed=moved // 4, transcendentals=0),
    )(*order, *arrays)


def body(
    local_gap,
    previous,
    flexibility,
    schur,
    corner_flex,
    coarse_inverse,
    scaling,
    counts,
    matching,
    corner_map,
):
    gap = local_gap[0, 0]
    prior = previous[0, 0]
    flex = flexibility[0, 0]
    dirichlet = schur[0, 0]
    weights = scaling[0, 0][None, :]
    rows, width = gap.shape
    face = width // 4
    corner_count = corner_flex.shape[2]
    coarse_count = coarse_inverse.shape[1]
    groups = core_groups(lax.axis_size("blk"), lax.axis_size("sector"))
    members = len(groups[0])
    odd_b = lax.rem(lax.axis_index("blk"), 2)
    odd_s = lax.rem(lax.axis_index("sector"), 2)

    chunk = coarse_inverse.shape[0]
    padded = (chunk + 7) // 8 * 8
    coarse_padded = coarse_count // chunk * padded
    own_rows = coarse_inverse.reshape(chunk, coarse_count // chunk, chunk)
    own_rows = jnp.pad(own_rows, ((0, padded - chunk), (0, 0), (0, padded - chunk)))
    own_rows = own_rows.reshape(padded, coarse_padded)
    full_inverse = lax.all_gather(own_rows, "sector", axis=0, tiled=True)

    order = jnp.stack([1 - odd_b, odd_b, 3 - odd_s, 2 + odd_s]).astype(jnp.int32)

    def exchange(links):
        b0, b1, s0, s1 = links
        s1 = swap(s1, "sector", 1)
        s0 = swap(s0, "sector", 0)
        b1 = swap(b1, "blk", 1)
        b0 = swap(b0, "blk", 0)
        return [b0, b1, s0, s1]

    own_map = corner_map[0, 0]
    own_map = (own_map // chunk * padded + lax.rem(own_map, chunk)).astype(F32)
    corners = jnp.pad(corner_flex[0, 0], ((0, SPAN - corner_count), (0, 0)))
    map_rows = jnp.full((8, face), -1.0, F32).at[0, :corner_count].set(own_map)
    came = call(
        first_kernel, [order], [prior, corners, map_rows], [(rows + SPAN + 8, face)] * 4, (), 10**6
    )
    came = exchange(came)

    active = (jnp.arange(face)[None, :] < counts[0, 0][:, None]).astype(F32)
    active_row = active.reshape(1, width)
    (picker,) = call(
        picker_kernel,
        [order],
        [matching[0, 0][None, :], active_row, flex, dirichlet],
        [jax.ShapeDtypeStruct((4, face, face), BF16)],
        (),
        10**8,
    )

    field_shape = (rows, width)
    link_shape = (rows, face)
    sums_shape = (coarse_padded // 2 + 8, LANES)
    square = jax.ShapeDtypeStruct((coarse_padded, coarse_padded), BF16)
    spots_shape = jax.ShapeDtypeStruct((2, coarse_padded, members * PAYLOAD), BF16)
    column_shape = (rows, LANES)
    faces_shape = jax.ShapeDtypeStruct((4, 2 * SPAN, face), BF16)
    taken_shape = jax.ShapeDtypeStruct((5 * SPAN, coarse_padded), BF16)
    big = 2 * rows * width * width
    slow = 8 * 10**9

    def flex_stage(mode, came, field, more):
        out = call(
            functools.partial(flex_kernel, mode),
            [order],
            list(came) + [field, picker, active_row, flex, corners] + more,
            [field_shape, field_shape]
            + [link_shape] * 4
            + [(PAYLOAD, LANES)]
            + [faces_shape, taken_shape] * (mode == 0),
            [pltpu.VMEM((2 * rows if mode == 2 else rows, width), BF16)],
            big,
        )
        return out[0], out[1], out[2:6], *out[6:]

    def gather(payload, links):
        many = jnp.broadcast_to(payload[None], (members, PAYLOAD, LANES))
        many = many.reshape(members * PAYLOAD, LANES)
        got = lax.all_to_all(
            many, BOTH, split_axis=0, concat_axis=0, tiled=True, axis_index_groups=groups
        )
        return got, exchange(links)

    def assemble(mode, *arrays):
        shapes = [sums_shape] + [spots_shape] * (mode == 0)
        kernel = functools.partial(assemble_kernel, mode)
        mine, *more = call(kernel, [], arrays, shapes, (), slow)
        return [mine, swap(mine, "blk", 0)], more

    def solve(mode, sums, *arrays):
        shapes = [(5 * SPAN, LANES)]
        if mode == 0:
            shapes += [square, square]
        if mode == 1:
            shapes += [column_shape, (coarse_padded, LANES), (8, LANES)]
        if mode == 2:
            shapes += [column_shape, column_shape]
        kernel = functools.partial(coarse_kernel, mode)
        return call(kernel, [], [*sums, taken, *arrays], shapes, (), slow)

    def schur_stage(mode, back, came, field, more):
        shapes = [field_shape, field_shape] + [link_shape] * 4
        if mode <= 1:
            shapes += [column_shape]
        if mode >= 1:
            shapes += [field_shape]
        if mode == 1:
            shapes += [field_shape]
        out = call(
            functools.partial(schur_kernel, mode),
            [order],
            [back, *came, field, picker, active_row, corner_faces, dirichlet, weights] + more,
            shapes,
            [pltpu.VMEM((rows, width), BF16)],
            big,
        )
        return out[0], out[1], out[2:6], out[6:]

    extra = jnp.zeros((8, rows), F32).at[3, :corner_count].set(own_map)
    start, field, links, payload, corner_faces, taken = flex_stage(
        0, came, prior, [gap, extra, map_rows]
    )
    got, came = gather(payload, links)
    places = got.reshape(members, PAYLOAD, LANES)[:, 11, rows : rows + corner_count]
    low = places[:, :PAYLOAD].reshape(-1)
    high = jnp.pad(
        places[:, PAYLOAD:], ((0, 0), (0, 2 * PAYLOAD - corner_count)), constant_values=-1.0
    )
    places = jnp.stack([low, high.reshape(-1)]).astype(jnp.int32)
    sums, (spots,) = assemble(0, got, places)
    back, head, rest = solve(0, sums, full_inverse)
    residual, weighted, links, (energy,) = schur_stage(0, back, came, field, [])

    came = exchange(links)
    direction, local, links, payload = flex_stage(1, came, weighted, [energy])
    got, came = gather(payload, links)
    sums, _ = assemble(1, got, spots)
    back, alpha, spread, sums = solve(1, sums, head, rest)
    residual, weighted, links, (energy, multipliers, image) = schur_stage(
        1, back, came, local, [alpha, residual, direction, start]
    )

    came = exchange(links)
    precond, local, links, payload = flex_stage(2, came, weighted, [energy, local])
    got, came = gather(payload, links)
    sums_2, _ = assemble(2, got, spots)
    back, alpha, beta = solve(2, sums_2, head, rest, spread, sums)
    residual, weighted, links, (multipliers,) = schur_stage(
        2, back, came, local, [alpha, residual, precond, multipliers, beta, image, direction]
    )
    came = exchange(links)
    (precond,) = call(
        last_kernel, [order], [*came, weighted, picker, active_row], [field_shape], (), big // 8
    )
    return (multipliers[None, None], residual[None, None], precond[None, None])


def solution(mesh):
    field = P("blk", "sector", None, None)
    vector = P("blk", "sector", None)
    placed = (field, field, field, field, field, P("sector", None), vector, vector, vector, vector)
    return jax.shard_map(
        body,
        mesh=mesh,
        in_specs=placed,
        out_specs=(field, field, field),
        check_vma=False,
    )
```

```python
import functools

import jax
import jax.numpy as jnp
from jax import lax
from jax.experimental import pallas as pl
from jax.experimental.pallas import tpu as pltpu
from jax.sharding import PartitionSpec as P

BOTH = ("blk", "sector")
PAYLOAD = 16
MAP_ROW = 11
LANES = 128
SPAN = 32
F32, BF16 = jnp.float32, jnp.bfloat16
VMEM_LIMIT = 12 * 1024 * 1024


def swap(block, axis, offset):
    count = lax.axis_size(axis)
    route = []
    for i in range(offset, count + offset, 2):
        one, two = i % count, (i + 1) % count
        route += [(one, two), (two, one)]
    return lax.ppermute(block, axis, route)


def core_groups(blk, sector):
    return [[b * sector + s for b in range(c, blk, 2) for s in range(sector)] for c in range(2)]


def parts_of(x, count):
    out = []
    for _ in range(count):
        head = x.astype(BF16)
        out.append(head)
        x = x - head.astype(F32)
    return out


def dot(a, b):
    return jnp.dot(a, b, preferred_element_type=F32)


def dot_nt(a, b):
    return lax.dot_general(a, b, (((1,), (1,)), ((), ())), preferred_element_type=F32)


def dot_tn(a, b):
    return lax.dot_general(a, b, (((0,), (0,)), ((), ())), preferred_element_type=F32)


def columns(order, link, face):
    return pl.ds(pl.multiple_of(order[link] * face, face), face)


def picked(came, picker, link, rows):
    stacked = jnp.concatenate(parts_of(came[link][0:rows, :], 3), axis=0)
    got = dot(stacked, picker[link])
    return got[:rows] + got[rows : 2 * rows] + got[2 * rows :]


def column(row, rows):
    return jnp.transpose(jnp.broadcast_to(row, (LANES, LANES)))[:rows]


def take_rows(taken, which, row):
    number = column(row, SPAN)
    lane = lax.broadcasted_iota(jnp.int32, (SPAN, LANES), 1).astype(F32)
    for at in range(0, taken.shape[1], LANES):
        hit = jnp.where(number == lane + float(at), 1.0, 0.0)
        taken[which * SPAN : (which + 1) * SPAN, at : at + LANES] = hit.astype(BF16)


def flex_kernel(mode, order, *refs):
    refs = list(refs)
    came = [refs.pop(0) for _ in range(4)]
    field, picker, active, flex, corners = [refs.pop(0) for _ in range(5)]
    if mode == 0:
        gap, numbers = refs.pop(0), refs.pop(0)
    if mode >= 1:
        energy = refs.pop(0)
    if mode == 2:
        old = refs.pop(0)
    p_out, h_out = refs.pop(0), refs.pop(0)
    links = [refs.pop(0) for _ in range(4)]
    if mode == 0:
        corner_faces, taken = refs.pop(1), refs.pop(1)
    payload, stack = refs
    rows, width = field.shape
    face = width // 4
    for link in range(4):
        cols = columns(order, link, face)
        p = field[:, cols] * active[:, cols] - picked(came, picker, link, rows)
        if mode == 0:
            p = 0.5 * p
        p_out[:, cols] = p
        if mode == 2:
            head, rest = parts_of(p, 2)
            stack[0:rows, cols] = head
            stack[rows : 2 * rows, cols] = rest
        else:
            stack[:, cols] = p.astype(BF16)
    if mode == 0:
        take_rows(taken, 0, numbers[0:1, 0:LANES])
        for link in range(4):
            cols = columns(order, link, face)
            own = corners[:, cols].astype(F32) * active[:, cols]
            theirs = dot(came[link][rows : rows + SPAN, :].astype(BF16), picker[link])
            corner_faces[link, 0:SPAN, :] = own.astype(BF16)
            corner_faces[link, SPAN : 2 * SPAN, :] = (-theirs).astype(BF16)
            take_rows(taken, link + 1, came[link][rows + SPAN : rows + SPAN + 1, 0:LANES])
    part = dot_nt(corners[...], stack[...])
    inner = jnp.zeros((rows, 1), F32)
    cross = jnp.zeros((rows, 1), F32)
    for link in range(4):
        cols = columns(order, link, face)
        local = dot(stack[...], flex[:, cols])
        if mode == 2:
            local = local[:rows] + local[rows:]
        p = p_out[:, cols]
        if mode == 0:
            local = gap[:, cols] - local
        else:
            inner = inner + jnp.sum(p * local, axis=1, keepdims=True)
        if mode == 2:
            cross = cross + jnp.sum(p * old[:, cols], axis=1, keepdims=True)
        h_out[:, cols] = local
        links[link][...] = local
    if mode == 2:
        part = part[:, :rows] + part[:, rows:]
    payload[0:16, 0:rows] = part[0:16]
    payload[0:8, rows : 2 * rows] = part[16:24]
    if mode == 0:
        at = lax.broadcasted_iota(jnp.int32, (8, rows), 0)
        scalars = jnp.where(at == MAP_ROW - 8, numbers[0:1, 0:rows], 0.0)
    else:
        lane = lax.broadcasted_iota(jnp.int32, (rows, LANES), 1)
        table = jnp.where(lane == 0, energy[...], jnp.where(lane == 1, inner, 0.0))
        table = jnp.where(lane == 2, cross, table)
        scalars = jnp.transpose(table)[0:8]
    payload[8:16, rows : 2 * rows] = scalars


def first_kernel(order, prior, corner_flex, numbers, corners, *links):
    count, width = corner_flex.shape
    blank = jnp.zeros((SPAN - count, width), F32)
    full = jnp.concatenate([corner_flex[...].astype(F32), blank], axis=0)
    corners[...] = full.astype(BF16)
    rows, width = prior.shape
    face = width // 4
    for link in range(4):
        cols = columns(order, link, face)
        links[link][0:rows, :] = prior[:, cols]
        links[link][rows : rows + SPAN, :] = corners[:, cols].astype(F32)
        links[link][rows + SPAN :, :] = numbers[...]


def picker_kernel(order, matching, active, flex, dirichlet, picker):
    face = picker.shape[1]
    source = lax.broadcasted_iota(jnp.int32, (face, face), 0)
    for link in range(4):
        cols = columns(order, link, face)
        hit = (source == matching[:, cols]) & (active[:, cols] > 0.5)
        picker[link] = jnp.where(hit, 1.0, 0.0).astype(BF16)


def assemble_kernel(mode, *refs):
    if mode == 0:
        got, out, spots = refs
        members, count = got.shape[0] // PAYLOAD, got.shape[0]
        maps = pltpu.roll(got[pl.ds(MAP_ROW, members, stride=PAYLOAD), :], LANES // 2, 1)
        maps = jnp.concatenate(parts_of(maps, 2), axis=0)
        lane = lax.broadcasted_iota(jnp.int32, (LANES, count), 0)
        slot = lax.broadcasted_iota(jnp.int32, (LANES, count), 1) & (PAYLOAD - 1)
        member = lax.broadcasted_iota(jnp.int32, (members, count), 0) * PAYLOAD
        gap = lax.broadcasted_iota(jnp.int32, (members, count), 1) - member
        own = (gap >= 0) & (gap < PAYLOAD)
        source = lax.broadcasted_iota(jnp.int32, (LANES, count), 0).astype(F32)
        for which in range(2):
            pickup = jnp.where(lane == slot + which * PAYLOAD, 1.0, 0.0).astype(BF16)
            number = dot(maps, pickup)
            number = jnp.where(own, number[:members] + number[members:], 0.0)
            number = jnp.sum(number, axis=0, keepdims=True)
            for at in range(0, spots.shape[1], LANES):
                hit = jnp.where(source + float(at) == number, 1.0, 0.0)
                spots[which, at : at + LANES, :] = hit.astype(BF16)
    else:
        got, spots, out = refs
    members = got.shape[0] // PAYLOAD
    half = spots.shape[1] // 2
    both = jnp.concatenate(parts_of(got[:, 0:LANES], 2), axis=1)
    low = dot(spots[0], both)
    high = dot(spots[1], both)
    low = low[:, :LANES] + low[:, LANES:]
    high = high[:, :LANES] + high[:, LANES:]
    spread = low + pltpu.roll(high, LANES // 2, 1)
    lane = lax.broadcasted_iota(jnp.int32, (half, LANES), 1)
    out[0:half, :] = jnp.where(
        lane < LANES // 2, spread[:half], pltpu.roll(spread[half:], LANES // 2, 1)
    )
    total = jnp.sum(got[:, 0:LANES].reshape(members, PAYLOAD, LANES), axis=0)
    out[half : half + 8, :] = total[8:16]


def coarse_kernel(mode, *refs):
    refs = list(refs)
    mine, theirs, taken = refs.pop(0), refs.pop(0), refs.pop(0)
    if mode == 0:
        inverse, back_out, head, rest = refs
        for at in range(0, inverse.shape[0], LANES):
            one, two = parts_of(inverse[at : at + LANES, :], 2)
            head[at : at + LANES, :] = one
            rest[at : at + LANES, :] = two
    else:
        head, rest = refs.pop(0), refs.pop(0)
    if mode == 1:
        back_out, alpha_out, spread_out, sums_out = refs
    if mode == 2:
        spread_old, sums_old, back_out, alpha_out, beta_out = refs
    rows = LANES // 2
    count = taken.shape[1]
    half = count // 2
    shift = LANES // 2
    total = mine[...] + theirs[...]
    spread = jnp.concatenate([total[:half], pltpu.roll(total[:half], shift, 1)], axis=0)
    sums = pltpu.roll(total[half:], shift, 1)
    valid = lax.broadcasted_iota(jnp.int32, (count, LANES), 1) < shift
    valid_row = lax.broadcasted_iota(jnp.int32, (1, LANES), 1) < shift
    spread = jnp.where(valid, spread, 0.0)
    if mode >= 1:
        energy, inner = sums[0:1], sums[1:2]
    if mode == 1:
        spread_out[...] = spread
        sums_out[...] = sums
    if mode == 2:
        beta = jnp.where(valid_row, energy / sums_old[0:1, :], 0.0)
        spread = spread + beta * spread_old[...]
        inner = inner + beta * (2.0 * sums[2:3] + beta * sums_old[1:2, :])
        beta_out[...] = column(beta, rows)
    first = spread.astype(BF16)
    second = spread - first.astype(F32)
    pair = (first.astype(F32) + pltpu.roll(second, shift, 1)).astype(BF16)
    coarse = dot(head[...], pair)
    coarse = coarse + pltpu.roll(coarse, shift, 1) + dot(rest[...], first)
    coarse = jnp.where(valid, coarse, 0.0)
    if mode >= 1:
        quad = jnp.sum(spread * coarse, axis=0, keepdims=True)
        alpha_out[...] = column(jnp.where(valid_row, energy / (inner + quad), 0.0), rows)
    one, two, three = parts_of(coarse, 3)
    pair = (one.astype(F32) + pltpu.roll(two.astype(F32), shift, 1)).astype(BF16)
    back = dot(taken[...], jnp.concatenate([pair, three], axis=1))
    low = back[:, :LANES]
    back_out[...] = low + pltpu.roll(low, shift, 1) + back[:, LANES:]


def schur_kernel(mode, order, *refs):
    refs = list(refs)
    back = refs.pop(0)
    came = [refs.pop(0) for _ in range(4)]
    field, picker, active, corner_faces, dirichlet, weights = [refs.pop(0) for _ in range(6)]
    if mode >= 1:
        alpha, before, direction, multipliers = [refs.pop(0) for _ in range(4)]
        alpha = alpha[:, 0:1]
    if mode == 2:
        beta, image_old, old = [refs.pop(0) for _ in range(3)]
        beta = beta[:, 0:1]
    residual, weighted = refs.pop(0), refs.pop(0)
    links = [refs.pop(0) for _ in range(4)]
    if mode <= 1:
        energy_out = refs.pop(0)
    if mode >= 1:
        mult_out = refs.pop(0)
    if mode == 1:
        image_out = refs.pop(0)
    (scaled,) = refs
    rows, width = field.shape
    face = width // 4
    back = back[...][:, :rows].astype(BF16)

    for link in range(4):
        cols = columns(order, link, face)
        jumped = field[:, cols] * active[:, cols] - picked(came, picker, link, rows)
        pieces = [back[0:SPAN], back[(link + 1) * SPAN : (link + 2) * SPAN]]
        behind = dot_tn(jnp.concatenate(pieces, axis=0), corner_faces[link])
        if mode == 0:
            now = jumped - behind
        else:
            d = direction[:, cols]
            if mode == 1:
                image_out[:, cols] = jumped
            else:
                jumped = jumped + beta * image_old[:, cols]
                d = d + beta * old[:, cols]
            mult_out[:, cols] = multipliers[:, cols] + alpha * d
            now = before[:, cols] - alpha * (jumped + behind)
        residual[:, cols] = now
        scaled[:, cols] = (now * weights[:, cols]).astype(BF16)
    energy = jnp.zeros((rows, 1), F32)
    for link in range(4):
        cols = columns(order, link, face)
        w = dot(scaled[...], dirichlet[:, cols]) * weights[:, cols]
        weighted[:, cols] = w
        links[link][...] = w
        if mode <= 1:
            energy = energy + jnp.sum(residual[:, cols] * w, axis=1, keepdims=True)
    if mode <= 1:
        energy_out[...] = jnp.broadcast_to(energy, (rows, LANES))


def last_kernel(order, *refs):
    came, (field, picker, active, out) = refs[:4], refs[4:]
    rows, width = field.shape
    for link in range(4):
        cols = columns(order, link, width // 4)
        out[:, cols] = field[:, cols] * active[:, cols] - picked(came, picker, link, rows)


def call(kernel, order, arrays, shapes, scratch=(), flops=0):
    where = pl.BlockSpec(memory_space=pltpu.VMEM)
    moved = sum(a.size * a.dtype.itemsize for a in arrays)
    return pl.pallas_call(
        kernel,
        out_shape=[s if hasattr(s, "dtype") else jax.ShapeDtypeStruct(s, F32) for s in shapes],
        in_specs=[pl.BlockSpec(memory_space=pltpu.SMEM)] * len(order) + [where] * len(arrays),
        out_specs=[where] * len(shapes),
        scratch_shapes=list(scratch),
        compiler_params=pltpu.CompilerParams(vmem_limit_bytes=VMEM_LIMIT),
        cost_estimate=pl.CostEstimate(flops=flops, bytes_accessed=moved // 4, transcendentals=0),
    )(*order, *arrays)


def body(
    local_gap,
    previous,
    flexibility,
    schur,
    corner_flex,
    coarse_inverse,
    scaling,
    counts,
    matching,
    corner_map,
):
    gap = local_gap[0, 0]
    prior = previous[0, 0]
    flex = flexibility[0, 0]
    dirichlet = schur[0, 0]
    weights = scaling[0, 0][None, :]
    rows, width = gap.shape
    face = width // 4
    corner_count = corner_flex.shape[2]
    coarse_count = coarse_inverse.shape[1]
    groups = core_groups(lax.axis_size("blk"), lax.axis_size("sector"))
    members = len(groups[0])
    odd_b = lax.rem(lax.axis_index("blk"), 2)
    odd_s = lax.rem(lax.axis_index("sector"), 2)

    chunk = coarse_inverse.shape[0]
    padded = (chunk + 7) // 8 * 8
    coarse_padded = coarse_count // chunk * padded
    own_rows = coarse_inverse.reshape(chunk, coarse_count // chunk, chunk)
    own_rows = jnp.pad(own_rows, ((0, padded - chunk), (0, 0), (0, padded - chunk)))
    own_rows = own_rows.reshape(padded, coarse_padded)
    full_inverse = lax.all_gather(own_rows, "sector", axis=0, tiled=True)

    order = jnp.stack([1 - odd_b, odd_b, 3 - odd_s, 2 + odd_s]).astype(jnp.int32)

    def exchange(links):
        b0, b1, s0, s1 = links
        s1 = swap(s1, "sector", 1)
        s0 = swap(s0, "sector", 0)
        b1 = swap(b1, "blk", 1)
        b0 = swap(b0, "blk", 0)
        return [b0, b1, s0, s1]

    own_map = corner_map[0, 0]
    own_map = (own_map // chunk * padded + lax.rem(own_map, chunk)).astype(F32)
    map_rows = jnp.full((8, face), -1.0, F32).at[0, :corner_count].set(own_map)
    corners, *links = call(
        first_kernel,
        [order],
        [prior, corner_flex[0, 0], map_rows],
        [jax.ShapeDtypeStruct((SPAN, width), BF16)] + [(rows + SPAN + 8, face)] * 4,
        (),
        10**6,
    )
    came = exchange(links)

    active = (jnp.arange(face)[None, :] < counts[0, 0][:, None]).astype(F32)
    active_row = active.reshape(1, width)
    (picker,) = call(
        picker_kernel,
        [order],
        [matching[0, 0][None, :], active_row, flex, dirichlet],
        [jax.ShapeDtypeStruct((4, face, face), BF16)],
        (),
        10**8,
    )

    field_shape = (rows, width)
    link_shape = (rows, face)
    sums_shape = (coarse_padded // 2 + 8, LANES)
    square = jax.ShapeDtypeStruct((coarse_padded, coarse_padded), BF16)
    spots_shape = jax.ShapeDtypeStruct((2, coarse_padded, members * PAYLOAD), BF16)
    column_shape = (rows, LANES)
    faces_shape = jax.ShapeDtypeStruct((4, 2 * SPAN, face), BF16)
    taken_shape = jax.ShapeDtypeStruct((5 * SPAN, coarse_padded), BF16)
    big = 2 * rows * width * width
    slow = 8 * 10**9

    def flex_stage(mode, came, field, more):
        out = call(
            functools.partial(flex_kernel, mode),
            [order],
            list(came) + [field, picker, active_row, flex, corners] + more,
            [field_shape, field_shape]
            + [link_shape] * 4
            + [(PAYLOAD, LANES)]
            + [faces_shape, taken_shape] * (mode == 0),
            [pltpu.VMEM((2 * rows if mode == 2 else rows, width), BF16)],
            big,
        )
        return out[0], out[1], out[2:6], *out[6:]

    def gather(payload, links):
        many = jnp.broadcast_to(payload[None], (members,) + payload.shape)
        many = many.reshape(members * PAYLOAD, payload.shape[1])
        got = lax.all_to_all(
            many, BOTH, split_axis=0, concat_axis=0, tiled=True, axis_index_groups=groups
        )
        return got, exchange(links)

    def assemble(mode, *arrays):
        shapes = [sums_shape] + [spots_shape] * (mode == 0)
        kernel = functools.partial(assemble_kernel, mode)
        mine, *more = call(kernel, [], arrays, shapes, (), slow)
        return [mine, swap(mine, "blk", 0)], more

    def solve(mode, sums, *arrays):
        shapes = [(5 * SPAN, LANES)]
        if mode == 0:
            shapes += [square, square]
        if mode == 1:
            shapes += [column_shape, (coarse_padded, LANES), (8, LANES)]
        if mode == 2:
            shapes += [column_shape, column_shape]
        kernel = functools.partial(coarse_kernel, mode)
        return call(kernel, [], [*sums, taken, *arrays], shapes, (), slow)

    def schur_stage(mode, back, came, field, more):
        shapes = [field_shape, field_shape] + [link_shape] * 4
        if mode <= 1:
            shapes += [column_shape]
        if mode >= 1:
            shapes += [field_shape]
        if mode == 1:
            shapes += [field_shape]
        out = call(
            functools.partial(schur_kernel, mode),
            [order],
            [back, *came, field, picker, active_row, corner_faces, dirichlet, weights] + more,
            shapes,
            [pltpu.VMEM((rows, width), BF16)],
            big,
        )
        return out[0], out[1], out[2:6], out[6:]

    start, field, links, payload, corner_faces, taken = flex_stage(
        0, came, prior, [gap, map_rows]
    )
    got, came = gather(payload, links)
    sums, (spots,) = assemble(0, got)
    back, head, rest = solve(0, sums, full_inverse)
    residual, weighted, links, (energy,) = schur_stage(0, back, came, field, [])

    came = exchange(links)
    direction, local, links, payload = flex_stage(1, came, weighted, [energy])
    got, came = gather(payload, links)
    sums, _ = assemble(1, got, spots)
    back, alpha, spread, sums = solve(1, sums, head, rest)
    residual, weighted, links, (energy, multipliers, image) = schur_stage(
        1, back, came, local, [alpha, residual, direction, start]
    )

    came = exchange(links)
    precond, local, links, payload = flex_stage(2, came, weighted, [energy, local])
    got, came = gather(payload, links)
    sums_2, _ = assemble(2, got, spots)
    back, alpha, beta = solve(2, sums_2, head, rest, spread, sums)
    residual, weighted, links, (multipliers,) = schur_stage(
        2, back, came, local, [alpha, residual, precond, multipliers, beta, image, direction]
    )
    came = exchange(links)
    (precond,) = call(
        last_kernel, [order], [*came, weighted, picker, active_row], [field_shape], (), big // 8
    )
    return (multipliers[None, None], residual[None, None], precond[None, None])


def solution(mesh):
    field = P("blk", "sector", None, None)
    vector = P("blk", "sector", None)
    placed = (field, field, field, field, field, P("sector", None), vector, vector, vector, vector)
    return jax.shard_map(
        body,
        mesh=mesh,
        in_specs=placed,
        out_specs=(field, field, field),
        check_vma=False,
    )
```

```python
import functools

import jax
import jax.numpy as jnp
from jax import lax
from jax.experimental import pallas as pl
from jax.experimental.pallas import tpu as pltpu
from jax.sharding import PartitionSpec as P

BOTH = ("blk", "sector")
PAYLOAD = 16
MAP_ROW = 11
LANES = 128
SPAN = 32
F32, BF16 = jnp.float32, jnp.bfloat16
VMEM_LIMIT = 12 * 1024 * 1024


def swap(block, axis, offset):
    count = lax.axis_size(axis)
    route = []
    for i in range(offset, count + offset, 2):
        one, two = i % count, (i + 1) % count
        route += [(one, two), (two, one)]
    return lax.ppermute(block, axis, route)


def core_groups(blk, sector):
    return [[b * sector + s for b in range(c, blk, 2) for s in range(sector)] for c in range(2)]


def parts_of(x, count):
    out = []
    for _ in range(count):
        head = x.astype(BF16)
        out.append(head)
        x = x - head.astype(F32)
    return out


def dot(a, b):
    return jnp.dot(a, b, preferred_element_type=F32)


def dot_nt(a, b):
    return lax.dot_general(a, b, (((1,), (1,)), ((), ())), preferred_element_type=F32)


def dot_tn(a, b):
    return lax.dot_general(a, b, (((0,), (0,)), ((), ())), preferred_element_type=F32)


def columns(order, link, face):
    return pl.ds(pl.multiple_of(order[link] * face, face), face)


def picked(came, picker, link, rows):
    stacked = jnp.concatenate(parts_of(came[link][0:rows, :], 2), axis=0)
    got = dot(stacked, picker[link])
    return got[:rows] + got[rows:]


def column(row, rows):
    return jnp.transpose(jnp.broadcast_to(row, (LANES, LANES)))[:rows]


def take_rows(taken, which, row):
    number = column(row, SPAN)
    lane = lax.broadcasted_iota(jnp.int32, (SPAN, LANES), 1).astype(F32)
    for at in range(0, taken.shape[1], LANES):
        hit = jnp.where(number == lane + float(at), 1.0, 0.0)
        taken[which * SPAN : (which + 1) * SPAN, at : at + LANES] = hit.astype(BF16)


def flex_kernel(mode, order, *refs):
    refs = list(refs)
    came = [refs.pop(0) for _ in range(4)]
    field, picker, active, flex, corners = [refs.pop(0) for _ in range(5)]
    if mode == 0:
        gap, numbers = refs.pop(0), refs.pop(0)
    if mode >= 1:
        energy = refs.pop(0)
    if mode == 2:
        old = refs.pop(0)
    p_out, h_out = refs.pop(0), refs.pop(0)
    links = [refs.pop(0) for _ in range(4)]
    if mode == 0:
        corner_faces, taken = refs.pop(1), refs.pop(1)
    payload, stack = refs
    rows, width = field.shape
    face = width // 4
    for link in range(4):
        cols = columns(order, link, face)
        p = field[:, cols] * active[:, cols] - picked(came, picker, link, rows)
        if mode == 0:
            p = 0.5 * p
        p_out[:, cols] = p
        if mode == 2:
            head, rest = parts_of(p, 2)
            stack[0:rows, cols] = head
            stack[rows : 2 * rows, cols] = rest
        else:
            stack[:, cols] = p.astype(BF16)
    if mode == 0:
        take_rows(taken, 0, numbers[0:1, 0:LANES])
        for link in range(4):
            cols = columns(order, link, face)
            own = corners[:, cols].astype(F32) * active[:, cols]
            theirs = dot(came[link][rows : rows + SPAN, :].astype(BF16), picker[link])
            corner_faces[link, 0:SPAN, :] = own.astype(BF16)
            corner_faces[link, SPAN : 2 * SPAN, :] = (-theirs).astype(BF16)
            take_rows(taken, link + 1, came[link][rows + SPAN : rows + SPAN + 1, 0:LANES])
    part = dot_nt(corners[...], stack[...])
    inner = jnp.zeros((rows, 1), F32)
    cross = jnp.zeros((rows, 1), F32)
    for link in range(4):
        cols = columns(order, link, face)
        local = dot(stack[...], flex[:, cols])
        if mode == 2:
            local = local[:rows] + local[rows:]
        p = p_out[:, cols]
        if mode == 0:
            local = gap[:, cols] - local
        else:
            inner = inner + jnp.sum(p * local, axis=1, keepdims=True)
        if mode == 2:
            cross = cross + jnp.sum(p * old[:, cols], axis=1, keepdims=True)
        h_out[:, cols] = local
        links[link][...] = local
    if mode == 2:
        part = part[:, :rows] + part[:, rows:]
    payload[0:16, 0:rows] = part[0:16]
    payload[0:8, rows : 2 * rows] = part[16:24]
    if mode == 0:
        at = lax.broadcasted_iota(jnp.int32, (8, rows), 0)
        scalars = jnp.where(at == MAP_ROW - 8, numbers[0:1, 0:rows], 0.0)
    else:
        lane = lax.broadcasted_iota(jnp.int32, (rows, LANES), 1)
        table = jnp.where(lane == 0, energy[...], jnp.where(lane == 1, inner, 0.0))
        table = jnp.where(lane == 2, cross, table)
        scalars = jnp.transpose(table)[0:8]
    payload[8:16, rows : 2 * rows] = scalars


def first_kernel(order, prior, corner_flex, numbers, corners, *links):
    count, width = corner_flex.shape
    blank = jnp.zeros((SPAN - count, width), F32)
    full = jnp.concatenate([corner_flex[...].astype(F32), blank], axis=0)
    corners[...] = full.astype(BF16)
    rows, width = prior.shape
    face = width // 4
    for link in range(4):
        cols = columns(order, link, face)
        links[link][0:rows, :] = prior[:, cols]
        links[link][rows : rows + SPAN, :] = corners[:, cols].astype(F32)
        links[link][rows + SPAN :, :] = numbers[...]


def picker_kernel(order, matching, active, flex, dirichlet, picker):
    face = picker.shape[1]
    source = lax.broadcasted_iota(jnp.int32, (face, face), 0)
    for link in range(4):
        cols = columns(order, link, face)
        hit = (source == matching[:, cols]) & (active[:, cols] > 0.5)
        picker[link] = jnp.where(hit, 1.0, 0.0).astype(BF16)


def assemble_kernel(mode, *refs):
    if mode == 0:
        got, out, spots = refs
        members, count = got.shape[0] // PAYLOAD, got.shape[0]
        maps = pltpu.roll(got[pl.ds(MAP_ROW, members, stride=PAYLOAD), :], LANES // 2, 1)
        maps = jnp.concatenate(parts_of(maps, 2), axis=0)
        lane = lax.broadcasted_iota(jnp.int32, (LANES, count), 0)
        slot = lax.broadcasted_iota(jnp.int32, (LANES, count), 1) & (PAYLOAD - 1)
        member = lax.broadcasted_iota(jnp.int32, (members, count), 0) * PAYLOAD
        gap = lax.broadcasted_iota(jnp.int32, (members, count), 1) - member
        own = (gap >= 0) & (gap < PAYLOAD)
        source = lax.broadcasted_iota(jnp.int32, (LANES, count), 0).astype(F32)
        for which in range(2):
            pickup = jnp.where(lane == slot + which * PAYLOAD, 1.0, 0.0).astype(BF16)
            number = dot(maps, pickup)
            number = jnp.where(own, number[:members] + number[members:], 0.0)
            number = jnp.sum(number, axis=0, keepdims=True)
            for at in range(0, spots.shape[1], LANES):
                hit = jnp.where(source + float(at) == number, 1.0, 0.0)
                spots[which, at : at + LANES, :] = hit.astype(BF16)
    else:
        got, spots, out = refs
    members = got.shape[0] // PAYLOAD
    half = spots.shape[1] // 2
    both = jnp.concatenate(parts_of(got[:, 0:LANES], 2), axis=1)
    low = dot(spots[0], both)
    high = dot(spots[1], both)
    low = low[:, :LANES] + low[:, LANES:]
    high = high[:, :LANES] + high[:, LANES:]
    spread = low + pltpu.roll(high, LANES // 2, 1)
    lane = lax.broadcasted_iota(jnp.int32, (half, LANES), 1)
    out[0:half, :] = jnp.where(
        lane < LANES // 2, spread[:half], pltpu.roll(spread[half:], LANES // 2, 1)
    )
    total = jnp.sum(got[:, 0:LANES].reshape(members, PAYLOAD, LANES), axis=0)
    out[half : half + 8, :] = total[8:16]


def coarse_kernel(mode, *refs):
    refs = list(refs)
    mine, theirs, taken = refs.pop(0), refs.pop(0), refs.pop(0)
    if mode == 0:
        inverse, back_out, head, rest = refs
        for at in range(0, inverse.shape[0], LANES):
            one, two = parts_of(inverse[at : at + LANES, :], 2)
            head[at : at + LANES, :] = one
            rest[at : at + LANES, :] = two
    else:
        head, rest = refs.pop(0), refs.pop(0)
    if mode == 1:
        back_out, alpha_out, spread_out, sums_out = refs
    if mode == 2:
        spread_old, sums_old, back_out, alpha_out, beta_out = refs
    rows = LANES // 2
    count = taken.shape[1]
    half = count // 2
    shift = LANES // 2
    total = mine[...] + theirs[...]
    spread = jnp.concatenate([total[:half], pltpu.roll(total[:half], shift, 1)], axis=0)
    sums = pltpu.roll(total[half:], shift, 1)
    valid = lax.broadcasted_iota(jnp.int32, (count, LANES), 1) < shift
    valid_row = lax.broadcasted_iota(jnp.int32, (1, LANES), 1) < shift
    spread = jnp.where(valid, spread, 0.0)
    if mode >= 1:
        energy, inner = sums[0:1], sums[1:2]
    if mode == 1:
        spread_out[...] = spread
        sums_out[...] = sums
    if mode == 2:
        beta = jnp.where(valid_row, energy / sums_old[0:1, :], 0.0)
        spread = spread + beta * spread_old[...]
        inner = inner + beta * (2.0 * sums[2:3] + beta * sums_old[1:2, :])
        beta_out[...] = column(beta, rows)
    first = spread.astype(BF16)
    second = spread - first.astype(F32)
    pair = (first.astype(F32) + pltpu.roll(second, shift, 1)).astype(BF16)
    coarse = dot(head[...], pair)
    coarse = coarse + pltpu.roll(coarse, shift, 1) + dot(rest[...], first)
    coarse = jnp.where(valid, coarse, 0.0)
    if mode >= 1:
        quad = jnp.sum(spread * coarse, axis=0, keepdims=True)
        alpha_out[...] = column(jnp.where(valid_row, energy / (inner + quad), 0.0), rows)
    one, two, three = parts_of(coarse, 3)
    pair = (one.astype(F32) + pltpu.roll(two.astype(F32), shift, 1)).astype(BF16)
    back = dot(taken[...], jnp.concatenate([pair, three], axis=1))
    low = back[:, :LANES]
    back_out[...] = low + pltpu.roll(low, shift, 1) + back[:, LANES:]


def schur_kernel(mode, order, *refs):
    refs = list(refs)
    back = refs.pop(0)
    came = [refs.pop(0) for _ in range(4)]
    field, picker, active, corner_faces, dirichlet, weights = [refs.pop(0) for _ in range(6)]
    if mode >= 1:
        alpha, before, direction, multipliers = [refs.pop(0) for _ in range(4)]
        alpha = alpha[:, 0:1]
    if mode == 2:
        beta, image_old, old = [refs.pop(0) for _ in range(3)]
        beta = beta[:, 0:1]
    residual, weighted = refs.pop(0), refs.pop(0)
    links = [refs.pop(0) for _ in range(4)]
    if mode <= 1:
        energy_out = refs.pop(0)
    if mode >= 1:
        mult_out = refs.pop(0)
    if mode == 1:
        image_out = refs.pop(0)
    (scaled,) = refs
    rows, width = field.shape
    face = width // 4
    back = back[...][:, :rows].astype(BF16)

    for link in range(4):
        cols = columns(order, link, face)
        jumped = field[:, cols] * active[:, cols] - picked(came, picker, link, rows)
        pieces = [back[0:SPAN], back[(link + 1) * SPAN : (link + 2) * SPAN]]
        behind = dot_tn(jnp.concatenate(pieces, axis=0), corner_faces[link])
        if mode == 0:
            now = jumped - behind
        else:
            d = direction[:, cols]
            if mode == 1:
                image_out[:, cols] = jumped
            else:
                jumped = jumped + beta * image_old[:, cols]
                d = d + beta * old[:, cols]
            mult_out[:, cols] = multipliers[:, cols] + alpha * d
            now = before[:, cols] - alpha * (jumped + behind)
        residual[:, cols] = now
        scaled[:, cols] = (now * weights[:, cols]).astype(BF16)
    energy = jnp.zeros((rows, 1), F32)
    for link in range(4):
        cols = columns(order, link, face)
        w = dot(scaled[...], dirichlet[:, cols]) * weights[:, cols]
        weighted[:, cols] = w
        links[link][...] = w
        if mode <= 1:
            energy = energy + jnp.sum(residual[:, cols] * w, axis=1, keepdims=True)
    if mode <= 1:
        energy_out[...] = jnp.broadcast_to(energy, (rows, LANES))


def last_kernel(order, *refs):
    came, (field, picker, active, out) = refs[:4], refs[4:]
    rows, width = field.shape
    for link in range(4):
        cols = columns(order, link, width // 4)
        out[:, cols] = field[:, cols] * active[:, cols] - picked(came, picker, link, rows)


def call(kernel, order, arrays, shapes, scratch=(), flops=0):
    where = pl.BlockSpec(memory_space=pltpu.VMEM)
    moved = sum(a.size * a.dtype.itemsize for a in arrays)
    return pl.pallas_call(
        kernel,
        out_shape=[s if hasattr(s, "dtype") else jax.ShapeDtypeStruct(s, F32) for s in shapes],
        in_specs=[pl.BlockSpec(memory_space=pltpu.SMEM)] * len(order) + [where] * len(arrays),
        out_specs=[where] * len(shapes),
        scratch_shapes=list(scratch),
        compiler_params=pltpu.CompilerParams(vmem_limit_bytes=VMEM_LIMIT),
        cost_estimate=pl.CostEstimate(flops=flops, bytes_accessed=moved // 4, transcendentals=0),
    )(*order, *arrays)


def body(
    local_gap,
    previous,
    flexibility,
    schur,
    corner_flex,
    coarse_inverse,
    scaling,
    counts,
    matching,
    corner_map,
):
    gap = local_gap[0, 0]
    prior = previous[0, 0]
    flex = flexibility[0, 0]
    dirichlet = schur[0, 0]
    weights = scaling[0, 0][None, :]
    rows, width = gap.shape
    face = width // 4
    corner_count = corner_flex.shape[2]
    coarse_count = coarse_inverse.shape[1]
    groups = core_groups(lax.axis_size("blk"), lax.axis_size("sector"))
    members = len(groups[0])
    odd_b = lax.rem(lax.axis_index("blk"), 2)
    odd_s = lax.rem(lax.axis_index("sector"), 2)

    chunk = coarse_inverse.shape[0]
    padded = (chunk + 7) // 8 * 8
    coarse_padded = coarse_count // chunk * padded
    own_rows = coarse_inverse.reshape(chunk, coarse_count // chunk, chunk)
    own_rows = jnp.pad(own_rows, ((0, padded - chunk), (0, 0), (0, padded - chunk)))
    own_rows = own_rows.reshape(padded, coarse_padded)
    full_inverse = lax.all_gather(own_rows, "sector", axis=0, tiled=True)

    order = jnp.stack([1 - odd_b, odd_b, 3 - odd_s, 2 + odd_s]).astype(jnp.int32)

    def exchange(links):
        b0, b1, s0, s1 = links
        s1 = swap(s1, "sector", 1)
        s0 = swap(s0, "sector", 0)
        b1 = swap(b1, "blk", 1)
        b0 = swap(b0, "blk", 0)
        return [b0, b1, s0, s1]

    own_map = corner_map[0, 0]
    own_map = (own_map // chunk * padded + lax.rem(own_map, chunk)).astype(F32)
    map_rows = jnp.full((8, face), -1.0, F32).at[0, :corner_count].set(own_map)
    corners, *links = call(
        first_kernel,
        [order],
        [prior, corner_flex[0, 0], map_rows],
        [jax.ShapeDtypeStruct((SPAN, width), BF16)] + [(rows + SPAN + 8, face)] * 4,
        (),
        10**6,
    )
    came = exchange(links)

    active = (jnp.arange(face)[None, :] < counts[0, 0][:, None]).astype(F32)
    active_row = active.reshape(1, width)
    (picker,) = call(
        picker_kernel,
        [order],
        [matching[0, 0][None, :], active_row, flex, dirichlet],
        [jax.ShapeDtypeStruct((4, face, face), BF16)],
        (),
        10**8,
    )

    field_shape = (rows, width)
    link_shape = (rows, face)
    sums_shape = (coarse_padded // 2 + 8, LANES)
    square = jax.ShapeDtypeStruct((coarse_padded, coarse_padded), BF16)
    spots_shape = jax.ShapeDtypeStruct((2, coarse_padded, members * PAYLOAD), BF16)
    column_shape = (rows, LANES)
    faces_shape = jax.ShapeDtypeStruct((4, 2 * SPAN, face), BF16)
    taken_shape = jax.ShapeDtypeStruct((5 * SPAN, coarse_padded), BF16)
    big = 2 * rows * width * width
    slow = 8 * 10**9

    def flex_stage(mode, came, field, more):
        out = call(
            functools.partial(flex_kernel, mode),
            [order],
            list(came) + [field, picker, active_row, flex, corners] + more,
            [field_shape, field_shape]
            + [link_shape] * 4
            + [(PAYLOAD, LANES)]
            + [faces_shape, taken_shape] * (mode == 0),
            [pltpu.VMEM((2 * rows if mode == 2 else rows, width), BF16)],
            big,
        )
        return out[0], out[1], out[2:6], *out[6:]

    def gather(payload, links):
        many = jnp.broadcast_to(payload[None], (members,) + payload.shape)
        many = many.reshape(members * PAYLOAD, payload.shape[1])
        got = lax.all_to_all(
            many, BOTH, split_axis=0, concat_axis=0, tiled=True, axis_index_groups=groups
        )
        return got, exchange(links)

    def assemble(mode, *arrays):
        shapes = [sums_shape] + [spots_shape] * (mode == 0)
        kernel = functools.partial(assemble_kernel, mode)
        mine, *more = call(kernel, [], arrays, shapes, (), slow)
        return [mine, swap(mine, "blk", 0)], more

    def solve(mode, sums, *arrays):
        shapes = [(5 * SPAN, LANES)]
        if mode == 0:
            shapes += [square, square]
        if mode == 1:
            shapes += [column_shape, (coarse_padded, LANES), (8, LANES)]
        if mode == 2:
            shapes += [column_shape, column_shape]
        kernel = functools.partial(coarse_kernel, mode)
        return call(kernel, [], [*sums, taken, *arrays], shapes, (), slow)

    def schur_stage(mode, back, came, field, more):
        shapes = [field_shape, field_shape] + [link_shape] * 4
        if mode <= 1:
            shapes += [column_shape]
        if mode >= 1:
            shapes += [field_shape]
        if mode == 1:
            shapes += [field_shape]
        out = call(
            functools.partial(schur_kernel, mode),
            [order],
            [back, *came, field, picker, active_row, corner_faces, dirichlet, weights] + more,
            shapes,
            [pltpu.VMEM((rows, width), BF16)],
            big,
        )
        return out[0], out[1], out[2:6], out[6:]

    start, field, links, payload, corner_faces, taken = flex_stage(
        0, came, prior, [gap, map_rows]
    )
    got, came = gather(payload, links)
    sums, (spots,) = assemble(0, got)
    back, head, rest = solve(0, sums, full_inverse)
    residual, weighted, links, (energy,) = schur_stage(0, back, came, field, [])

    came = exchange(links)
    direction, local, links, payload = flex_stage(1, came, weighted, [energy])
    got, came = gather(payload, links)
    sums, _ = assemble(1, got, spots)
    back, alpha, spread, sums = solve(1, sums, head, rest)
    residual, weighted, links, (energy, multipliers, image) = schur_stage(
        1, back, came, local, [alpha, residual, direction, start]
    )

    came = exchange(links)
    precond, local, links, payload = flex_stage(2, came, weighted, [energy, local])
    got, came = gather(payload, links)
    sums_2, _ = assemble(2, got, spots)
    back, alpha, beta = solve(2, sums_2, head, rest, spread, sums)
    residual, weighted, links, (multipliers,) = schur_stage(
        2, back, came, local, [alpha, residual, precond, multipliers, beta, image, direction]
    )
    came = exchange(links)
    (precond,) = call(
        last_kernel, [order], [*came, weighted, picker, active_row], [field_shape], (), big // 8
    )
    return (multipliers[None, None], residual[None, None], precond[None, None])


def solution(mesh):
    field = P("blk", "sector", None, None)
    vector = P("blk", "sector", None)
    placed = (field, field, field, field, field, P("sector", None), vector, vector, vector, vector)
    return jax.shard_map(
        body,
        mesh=mesh,
        in_specs=placed,
        out_specs=(field, field, field),
        check_vma=False,
    )
```
